32 devices in a mesh: seq: 16 (over z, y, x), tp: 2 (over core).
Axes of the slice: x: 2, y: 2, z: 4, core: 2. Of those that a mesh axis runs over, the one named last changes fastest.
Arguments:
- layer_input: bfloat16 [4096, 2048], P('seq'), may hold values from -1.5 to 1.5
- query: bfloat16 [4096, 2048], P('seq', 'tp'), may hold values from -6 to 6
- suffix_kv: bfloat16 [2, 4096, 2048], P(None, 'seq', 'tp'), may hold values from -6 to 6
- prefix_kv: bfloat16 [2, 512, 2048], P(None, 'seq', 'tp'), may hold values from -6 to 6
- node_len: int32 [16], replicated, may hold values from 8 to 32, as said below
- path: int32 [16, 3], P('seq'), may hold values from 0 to 15, as said below
- out_weight: bfloat16 [2048, 2048], P('tp'), may hold values from -0.125 to 0.125
- norm_gain: float32 [2048], replicated, may hold values from 0.1 to 1.9
- expert_ids: int32 [4096, 8], P('seq'), may hold values from 0 to 15, all different within a row; in each aligned block of 256 rows (0 to 255, 256 to 511, ...) at most 160 rows name the same one
- gates: float32 [4096, 8], P('seq'), may hold values from 0.1 to 0.4
- w_gate: bfloat16 [16, 2048, 1024], P('seq', None, 'tp'), may hold values from -0.125 to 0.125
- w_up: bfloat16 [16, 2048, 1024], P('seq', None, 'tp'), may hold values from -0.125 to 0.125
- w_down: bfloat16 [16, 1024, 2048], P('seq', 'tp'), may hold values from -0.1875 to 0.1875
Outputs:
- layer_out: bfloat16 [4096, 2048], P('seq', 'tp')
The draws below stay inside these ranges and needn't reach their ends.
Inputs may be any that keep to these rules, and one draw needn't show every extreme that they name: `path`: row r names three different nodes. Nodes are of three levels: roots, middle nodes and leaves; a middle node always comes with the same root, a leaf always with the same middle node, and every node is named by some request. `node_len`: some node holds exactly 32 tokens. `expert_ids`: within the 256 rows of one request no expert is named more than 160 times, a bound that some block reaches.
All inputs are finite; a program needn't handle non-finite values.
Results may differ from the reference program's by a relative error of at most 0.019.
Values may be sent and summed in bfloat16 or wider, within the bound.
A program may use at most 128 MiB of HBM per device.

```python
import math
import jax
import jax.numpy as jnp
import numpy as np
from jax import lax

D = 2048
HEADS = 16
HD = 128
FF = 1024
TOPK = 8
Q = 256
SLOT = 32
EXPERTS = 16
NODES = 16
REQ = 16
TOKENS = 4096
CAP = 160


def draw_query(key, part):
    base = jnp.clip(jax.random.normal(jax.random.fold_in(key, 1), (TOKENS, HEADS * HD), jnp.float32), -4.0, 4.0)
    return base.astype(jnp.bfloat16)


def draw_suffix_kv(key, part):
    base = jnp.clip(jax.random.normal(jax.random.fold_in(key, 3), (2, TOKENS, HEADS * HD), jnp.float32), -4.0, 4.0)
    return base.astype(jnp.bfloat16)


def draw_node_len(key, part):
    lens = jax.random.randint(jax.random.fold_in(key, 31), (NODES,), SLOT // 4, SLOT + 1)
    full = jax.random.randint(jax.random.fold_in(key, 32), (), 0, NODES)
    return jnp.where(jnp.arange(NODES) == full, SLOT, lens).astype(jnp.int32)


def draw_path(key, part):
    roots = NODES // 16
    middles = 3 * NODES // 16
    leaves = 12 * NODES // 16
    owner = jax.random.permutation(jax.random.fold_in(key, 21), NODES)
    extra = jax.random.randint(jax.random.fold_in(key, 23), (REQ - leaves,), 0, leaves)
    leaf_of = jnp.concatenate([jnp.arange(leaves), extra])
    order = jax.random.permutation(jax.random.fold_in(key, 22), REQ)
    leaf_of = leaf_of[order]
    middle_of = leaf_of // 4
    root_of = middle_of // 3
    return jnp.stack([owner[root_of], owner[roots + middle_of], owner[roots + middles + leaf_of]], 1).astype(jnp.int32)


def block_scale(own_key, shape, split, smallest, largest):
    def one(position, shards_of):
        steps = jax.random.uniform(jax.random.fold_in(jax.random.fold_in(own_key, 6), position), (shards_of,), jnp.float32, smallest / len(split), largest / len(split))
        return jnp.repeat(jnp.exp(steps), shape[position] // shards_of).reshape((-1,) + (1,) * (len(shape) - position - 1))

    loudness = one(*split[0])
    for cut in split[1:]:
        loudness = loudness * one(*cut)
    return loudness


def shared_out(rng, own, number, rows, count, top, bound, lean):
    sequence = jax.random.permutation(rng, count)
    packed, usual = load_shares(count, rows * top, bound, lean, True), load_shares(count, rows * top, bound, lean, False)
    places = jnp.arange(count)

    def named(lengths, turn):
        used = int((lengths > 0).sum())
        fixed = max(1, used // 4)
        shifted = fixed + (places - fixed + turn * (used - fixed)) % max(1, count - fixed)
        return jnp.zeros((count,), jnp.int32).at[sequence[jnp.where(places < fixed, places, shifted)]].set(jnp.asarray(lengths, jnp.int32))

    lengths = jnp.where(number % 4 == 0, named(packed, number // 4), named(usual, number - number // 4 - 1))
    mixed = jax.random.permutation(jax.random.fold_in(own, 3), count)
    giver, receiver = mixed[0:count // 2 * 2:2], mixed[1:count // 2 * 2:2]
    margin = jnp.minimum(lengths[giver] - 1, bound - lengths[receiver]) // 2
    margin = jnp.where((giver == sequence[0]) | (receiver == sequence[0]) | (lengths[receiver] == 0), 0, jnp.maximum(margin, 0))
    shifted = jax.random.randint(jax.random.fold_in(own, 4), (count // 2,), 0, 1 << 20) % (margin + 1)
    lengths = lengths.at[giver].add(-shifted).at[receiver].add(shifted)
    labels = jnp.searchsorted(jnp.cumsum(lengths), jnp.arange(rows * top), side="right").astype(jnp.int32)
    listing = labels.reshape(top, rows).T
    listing = listing[jax.random.permutation(jax.random.fold_in(own, 1), rows)]
    turn = jax.random.randint(jax.random.fold_in(own, 2), (rows, 1), 0, top)
    return jnp.take_along_axis(listing, (jnp.arange(top)[None, :] + turn) % top, axis=1)


def load_shares(number_of, total, bound, skew, full):
    weights = [(1 << 20) // math.isqrt(rank ** skew) + 1 for rank in range(1, number_of + 1)]
    largest = bound if full else min(bound, max(-(-total // number_of), total * weights[0] // sum(weights)))
    least = 1 if total - largest >= number_of - 1 else 0
    given, rest = [largest] + [least] * (number_of - 1), total - largest - least * (number_of - 1)
    while rest > 0:
        free = [i for i in range(1, number_of) if given[i] < largest] or [i for i in range(1, number_of) if given[i] < bound]
        pool, left = sum([weights[i] for i in free]), rest
        for i in free:
            more = min(bound - given[i], max(1, left * weights[i] // pool), rest)
            given[i] = given[i] + more
            rest = rest - more
    return np.array(given)


def centred(key, shape, scale, bound, split=(), held_as=jnp.bfloat16):
    gain = block_scale(key, shape, split, -0.22, 0.18) if split else 1.0
    entries = jax.random.normal(key, shape, jnp.float32) * scale * gain
    return jnp.minimum(jnp.maximum(entries, -bound), bound).astype(held_as)


def setup_inputs(seed: int = 0) -> dict:
    key_list = jax.random.split(jax.random.key(seed), 14)
    layer_input = centred(key_list[0], (TOKENS, D), 0.25, 1.5, ((0, 16),))
    query = draw_query(jax.random.fold_in(key_list[13], 71), 0)
    suffix_kv = draw_suffix_kv(jax.random.fold_in(key_list[13], 71), 0)
    prefix_kv = centred(key_list[3], (2, NODES * SLOT, HEADS * HD), 1.0, 6.0, ((1, 16), (2, 2)))
    node_len = draw_node_len(jax.random.fold_in(key_list[13], 71), 0)
    path = draw_path(jax.random.fold_in(key_list[13], 71), 0)
    out_weight = centred(key_list[6], (HEADS * HD, D), (HEADS * HD) ** -0.5, 0.125, ((0, 2),))
    norm_gain = jnp.clip(1.0 + 0.18 * jax.random.normal(key_list[7], (D,), jnp.float32), 0.1, 1.9)
    expert_ids_keys = jax.random.split(jax.random.fold_in(key_list[8], 1), TOKENS // Q)
    expert_ids_turns = jax.random.permutation(jax.random.fold_in(key_list[8], 3), TOKENS // Q)
    expert_ids = jax.vmap(lambda own, number: shared_out(jax.random.fold_in(key_list[8], 2), own, number, Q, EXPERTS, TOPK, CAP, 2))(expert_ids_keys, expert_ids_turns).reshape((TOKENS, TOPK))
    gates = jnp.clip(0.1 + 0.3 * jax.random.uniform(key_list[9], (TOKENS, TOPK), jnp.float32) ** block_scale(key_list[9], (TOKENS, TOPK), ((0, 16),), -0.2, 0.2), 0.1, 0.4)
    w_gate = centred(key_list[10], (EXPERTS, D, FF), D ** -0.5, 0.125, ((0, 16), (2, 2)))
    w_up = centred(key_list[11], (EXPERTS, D, FF), D ** -0.5, 0.125, ((0, 16), (2, 2)))
    w_down = centred(key_list[12], (EXPERTS, FF, D), FF ** -0.5, 0.1875, ((0, 16), (1, 2)))
    return dict(layer_input=layer_input, query=query, suffix_kv=suffix_kv, prefix_kv=prefix_kv, node_len=node_len, path=path, out_weight=out_weight, norm_gain=norm_gain, expert_ids=expert_ids, gates=gates, w_gate=w_gate, w_up=w_up, w_down=w_down)


def slot_plan(ids, experts, cap):
    flat = ids.reshape(-1)
    onehot = (flat[:, None] == jnp.arange(experts, dtype=jnp.int32)[None, :]).astype(jnp.int32)
    rank = lax.optimization_barrier(jnp.sum(jnp.cumsum(onehot, axis=0) * onehot, axis=1)) - 1
    return (flat * cap + rank).astype(jnp.int32)

def reference(layer_input, query, suffix_kv, prefix_kv, node_len, path, out_weight, norm_gain, expert_ids, gates, w_gate, w_up, w_down):
    width = HEADS * HD
    scale = 1.0 / math.sqrt(HD)
    prefix = prefix_kv.reshape(2, NODES, SLOT, width)
    positions = jnp.arange(SLOT, dtype=jnp.int32)

    def attend(item):
        queries, own_kv, nodes = item
        node_keys = prefix[0][nodes].reshape(3 * SLOT, width)
        node_values = prefix[1][nodes].reshape(3 * SLOT, width)
        live = (positions[None, :] < node_len[nodes][:, None]).reshape(-1)
        live_all = jnp.concatenate([jnp.ones((Q,), dtype=bool), live])
        keys = jnp.concatenate([own_kv[0], node_keys], 0).astype(jnp.float32).reshape(-1, HEADS, HD)
        values = jnp.concatenate([own_kv[1], node_values], 0).astype(jnp.float32).reshape(-1, HEADS, HD)
        scores = jnp.einsum('qhd,khd->hqk', queries.astype(jnp.float32).reshape(Q, HEADS, HD), keys) * scale
        scores = jnp.where(live_all[None, None, :], scores, -jnp.inf)
        weights = jax.nn.softmax(scores, axis=2)
        result = jnp.einsum('hqk,khd->qhd', weights, values)
        return result.reshape(Q, width).astype(jnp.bfloat16)
    blocks = (query.reshape(REQ, Q, width), suffix_kv.reshape(2, REQ, Q, width).transpose(1, 0, 2, 3), path)
    attn = lax.map(attend, blocks).reshape(TOKENS, width)
    hidden_state = layer_input.astype(jnp.float32) + jnp.dot(attn, out_weight, preferred_element_type=jnp.float32)
    mean_square = lax.optimization_barrier(jnp.mean(hidden_state * hidden_state, axis=1, keepdims=True))
    normed = (hidden_state * lax.rsqrt(mean_square + 1e-06) * norm_gain).astype(jnp.bfloat16)
    dest = jax.vmap(lambda ids: slot_plan(ids, EXPERTS, CAP))(expert_ids.reshape(REQ, Q, TOPK))
    pairs_all = TOKENS * TOPK
    pair_index = jnp.arange(pairs_all, dtype=jnp.int32).reshape(REQ, Q * TOPK)
    table = jnp.full((REQ, EXPERTS * CAP), pairs_all, dtype=jnp.int32)
    table = table.at[jnp.arange(REQ, dtype=jnp.int32)[:, None], dest].set(pair_index)
    table = table.reshape(REQ, EXPERTS, CAP).transpose(1, 0, 2).reshape(EXPERTS, REQ * CAP)
    gate_flat = gates.reshape(-1)

    def add_expert(accum, item):
        gate_w, up_w, down_w, pairs = item
        valid = pairs < pairs_all
        safe = jnp.minimum(pairs, pairs_all - 1)
        token = (safe // TOPK).astype(jnp.int32)
        rows = normed[token]
        gate_part = jnp.dot(rows, gate_w, preferred_element_type=jnp.float32)
        up_part = jnp.dot(rows, up_w, preferred_element_type=jnp.float32)
        act = (jax.nn.silu(gate_part) * up_part).astype(jnp.bfloat16)
        result = jnp.dot(act, down_w, preferred_element_type=jnp.float32).astype(jnp.bfloat16)
        result = lax.optimization_barrier(result).astype(jnp.float32)
        weight = jnp.where(valid, gate_flat[safe], jnp.zeros_like(gate_flat[safe]))
        return (accum.at[token].add(weight[:, None] * result), None)
    accum, _ = lax.scan(add_expert, jnp.zeros((TOKENS, D), jnp.float32), (w_gate, w_up, w_down, table))
    return (hidden_state + accum).astype(jnp.bfloat16)
```

```python
import math

import jax
import jax.numpy as jnp
from jax import lax
from jax.sharding import PartitionSpec as P

D = 2048
HD = 128
TOPK = 8
SLOT = 32
DENSE_SEQ = 16


def slot_plan(ids, experts, cap):
    flat = ids.reshape(-1)
    onehot = (flat[:, None] == jnp.arange(experts, dtype=jnp.int32)[None, :]).astype(jnp.int32)
    rank = jnp.sum(jnp.cumsum(onehot, axis=0) * onehot, axis=1) - 1
    return flat * cap + rank


def dense_experts(normed, expert_ids, gates, w_gate, w_up, w_down, tp_index, half):
    mine = lax.axis_index("seq")
    experts = lax.axis_size("seq")
    named = expert_ids[:, :, None] == jnp.arange(experts, dtype=jnp.int32)[None, None, :]
    table = jnp.sum(jnp.where(named, gates[:, :, None], 0.0), axis=1)
    table = lax.all_gather(table, "seq", axis=0, tiled=True)
    weight = lax.dynamic_slice_in_dim(table, mine, 1, 1)
    part = lax.dynamic_slice_in_dim(normed, tp_index * half, half, 1)
    column = lax.all_gather(part, "seq", axis=0, tiled=True)
    tokens = lax.all_gather(column, "tp", axis=1, tiled=True)
    gate_part = jnp.dot(tokens, w_gate[0], preferred_element_type=jnp.float32)
    up_part = jnp.dot(tokens, w_up[0], preferred_element_type=jnp.float32)
    act = (jax.nn.silu(gate_part) * up_part).astype(jnp.bfloat16)
    terms = jnp.dot(act, w_down[0], preferred_element_type=jnp.float32) * weight
    terms = lax.psum_scatter(terms.astype(jnp.bfloat16), "tp", scatter_dimension=1, tiled=True)
    return lax.psum_scatter(terms, "seq", scatter_dimension=0, tiled=True).astype(jnp.float32)


def local(
    layer_input,
    query,
    suffix_kv,
    prefix_kv,
    node_len,
    path,
    out_weight,
    norm_gain,
    expert_ids,
    gates,
    w_gate,
    w_up,
    w_down,
):
    rows = query.shape[0]
    heads_here = query.shape[1] // HD
    scale = 1.0 / math.sqrt(HD)
    queries = query.reshape(rows, heads_here, HD)
    own_keys = suffix_kv[0].reshape(rows, heads_here, HD)
    own_values = suffix_kv[1].reshape(rows, heads_here, HD).astype(jnp.float32)
    scores = (
        jnp.einsum("qhd,khd->hqk", queries, own_keys, preferred_element_type=jnp.float32) * scale
    )
    top = jnp.max(scores, axis=2)
    probs = jnp.exp(scores - top[:, :, None])
    total = jnp.sum(probs, axis=2)
    accum = jnp.einsum("hqk,khd->hqd", probs, own_values)
    my_nodes = path[0]
    node_ids = jnp.arange(node_len.shape[0], dtype=jnp.int32)
    piece = lax.all_gather(prefix_kv, "seq", axis=1, tiled=True)
    start = jnp.int32(0)
    count = piece.shape[1]

    def absorb(state):
        best, mass, sums = state
        index = jnp.arange(count, dtype=jnp.int32)
        node = index // SLOT
        offset = index % SLOT
        match = node[:, None] == node_ids[None, :]
        lengths = jnp.sum(jnp.where(match, node_len[None, :], 0), axis=1)
        live = (offset < lengths) & jnp.any(node[:, None] == my_nodes[None, :], axis=1)
        piece_keys = piece[0].reshape(count, heads_here, HD)
        piece_values = piece[1].reshape(count, heads_here, HD).astype(jnp.float32)
        block = (
            jnp.einsum("qhd,khd->hqk", queries, piece_keys, preferred_element_type=jnp.float32)
            * scale
        )
        block = jnp.where(live[None, None, :], block, -jnp.inf)
        new_best = jnp.maximum(best, jnp.max(block, axis=2))
        weights = jnp.exp(block - new_best[:, :, None])
        factor = jnp.exp(best - new_best)
        new_mass = mass * factor + jnp.sum(weights, axis=2)
        new_sums = sums * factor[:, :, None] + jnp.einsum("hqk,khd->hqd", weights, piece_values)
        return (new_best, new_mass, new_sums)

    node_start = my_nodes * SLOT
    touched = jnp.any((node_start + SLOT > start) & (node_start < start + count))
    top, total, accum = lax.cond(touched, absorb, lambda state: state, (top, total, accum))
    attn = (accum / total[:, :, None]).astype(jnp.bfloat16)
    partial_value = jnp.einsum(
        "hqd,hdm->qm",
        attn,
        out_weight.reshape(heads_here, HD, D),
        preferred_element_type=jnp.float32,
    )
    tp_index = lax.axis_index("tp")
    tp_count = lax.axis_size("tp")
    half = D // tp_count
    experts = w_gate.shape[0] * lax.axis_size("seq")
    cap = 5 * rows * TOPK // (4 * experts)
    dest = slot_plan(expert_ids, experts, cap)
    hidden_state = layer_input.astype(jnp.float32) + lax.psum(partial_value, "tp")
    mean_square = jnp.mean(hidden_state * hidden_state, axis=1, keepdims=True)
    normed = (hidden_state * lax.rsqrt(mean_square + 1e-06) * norm_gain).astype(jnp.bfloat16)
    if lax.axis_size("seq") <= DENSE_SEQ:
        mixture = dense_experts(normed, expert_ids, gates, w_gate, w_up, w_down, tp_index, half)
        residual = lax.dynamic_slice_in_dim(hidden_state, tp_index * half, half, 1)
        return (residual + mixture).astype(jnp.bfloat16)
    spread = jnp.repeat(normed, TOPK, axis=0)
    outgoing = (
        jnp.zeros((experts * cap, D), jnp.bfloat16).at[dest].set(spread).reshape(experts, cap, D)
    )
    arrived = lax.all_to_all(outgoing, "seq", split_axis=0, concat_axis=0, tiled=True)
    sources = arrived.shape[0]
    items = arrived.shape[1]
    flat = arrived.reshape(sources * items, D)
    gate_part = jnp.dot(flat, w_gate[0], preferred_element_type=jnp.float32)
    up_part = jnp.dot(flat, w_up[0], preferred_element_type=jnp.float32)
    act = (jax.nn.silu(gate_part) * up_part).astype(jnp.bfloat16)
    terms = jnp.dot(act, w_down[0], preferred_element_type=jnp.float32).reshape(sources, items, D)
    summed = lax.psum_scatter(terms, "tp", scatter_dimension=2, tiled=True).astype(jnp.bfloat16)
    back = lax.all_to_all(summed, "seq", split_axis=0, concat_axis=0, tiled=True)
    residual = lax.dynamic_slice_in_dim(hidden_state, tp_index * half, half, 1)
    results = back.reshape(experts * cap, half)[dest].reshape(rows, TOPK, half).astype(jnp.float32)
    mixture = jnp.sum(gates[:, :, None] * results, axis=1)
    return (residual + mixture).astype(jnp.bfloat16)


def solution(mesh):
    in_specs = (
        P("seq", None),
        P("seq", "tp"),
        P(None, "seq", "tp"),
        P(None, "seq", "tp"),
        P(),
        P("seq", None),
        P("tp", None),
        P(),
        P("seq", None),
        P("seq", None),
        P("seq", None, "tp"),
        P("seq", None, "tp"),
        P("seq", "tp", None),
    )
    out_specs = P("seq", "tp")
    return jax.shard_map(local, mesh=mesh, in_specs=in_specs, out_specs=out_specs, check_vma=False)
```

```python
import math

import jax
import jax.numpy as jnp
from jax import lax
from jax.sharding import PartitionSpec as P

D = 2048
HD = 128
TOPK = 8
SLOT = 32
DENSE_SEQ = 16


def slot_plan(ids, experts, cap):
    flat = ids.reshape(-1)
    onehot = (flat[:, None] == jnp.arange(experts, dtype=jnp.int32)[None, :]).astype(jnp.int32)
    rank = jnp.sum(jnp.cumsum(onehot, axis=0) * onehot, axis=1) - 1
    return flat * cap + rank


def flip(value, bit):
    return lax.ppermute(value, "seq", [(i, i ^ bit) for i in range(DENSE_SEQ)])


def shift(value, step):
    return lax.ppermute(value, "seq", [(i, (i + 4 * step) % DENSE_SEQ) for i in range(DENSE_SEQ)])


def gather_blocks(part):
    planes = jnp.stack([part] + [shift(part, k) for k in range(1, 4)])
    half = part.shape[-1] // 2
    first, second = planes[..., :half], planes[..., half:]
    first = jnp.stack([first, flip(first, 1)], 1)
    second = jnp.stack([second, flip(second, 2)], 1)
    first = jnp.stack([first, flip(first, 2)], 1)
    second = jnp.stack([second, flip(second, 1)], 2)
    return jnp.concatenate([first, second], -1)


def block_owners():
    mine = lax.axis_index("seq")
    return jnp.stack(
        [(mine + DENSE_SEQ - 4 * k) % DENSE_SEQ ^ b for k in range(4) for b in range(4)]
    )


def add(a, b):
    return (a.astype(jnp.float32) + b.astype(jnp.float32)).astype(jnp.bfloat16)


def reduce_blocks(terms):
    half = terms.shape[-1] // 2
    first, second = terms[..., :half], terms[..., half:]
    first_x = flip(first[:, :, 1], 1)
    second_y = flip(second[:, 1], 2)
    first = add(first[:, :, 0], first_x)
    second = add(second[:, 0], second_y)
    first_y = flip(first[:, 1], 2)
    second_x = flip(second[:, 1], 1)
    first = add(first[:, 0], first_y)
    second = add(second[:, 0], second_x)
    sums = []
    for piece in (first, second):
        arrived = [shift(piece[k], -k) for k in range(1, 4)]
        sums.append(piece[0].astype(jnp.float32) + sum(a.astype(jnp.float32) for a in arrived))
    return jnp.concatenate(sums, -1)


def dense_experts(normed, expert_ids, gates, w_gate, w_up, w_down, tp_index, half):
    mine = lax.axis_index("seq")
    experts = lax.axis_size("seq")
    rows = normed.shape[0]
    named = expert_ids[:, :, None] == jnp.arange(experts, dtype=jnp.int32)[None, None, :]
    table = jnp.sum(jnp.where(named, gates[:, :, None], 0.0), axis=1)
    table = lax.all_gather(table, "seq", axis=0, tiled=True)
    weight = lax.dynamic_slice_in_dim(table, mine, 1, 1)
    weight = weight.reshape(experts, -1)[block_owners()].reshape(-1, 1)
    part = lax.dynamic_slice_in_dim(normed, tp_index * half, half, 1)
    column = gather_blocks(part).reshape(experts * rows, half)
    tokens = lax.all_gather(column, "tp", axis=1, tiled=True)
    gate_part = jnp.dot(tokens, w_gate[0], preferred_element_type=jnp.float32)
    up_part = jnp.dot(tokens, w_up[0], preferred_element_type=jnp.float32)
    act = (jax.nn.silu(gate_part) * up_part).astype(jnp.bfloat16)
    terms = jnp.dot(act, w_down[0], preferred_element_type=jnp.float32) * weight
    terms = lax.psum_scatter(terms.astype(jnp.bfloat16), "tp", scatter_dimension=1, tiled=True)
    return reduce_blocks(terms.reshape(4, 2, 2, rows, half))


def local(
    layer_input,
    query,
    suffix_kv,
    prefix_kv,
    node_len,
    path,
    out_weight,
    norm_gain,
    expert_ids,
    gates,
    w_gate,
    w_up,
    w_down,
):
    rows = query.shape[0]
    heads_here = query.shape[1] // HD
    scale = 1.0 / math.sqrt(HD)
    queries = query.reshape(rows, heads_here, HD)
    own_keys = suffix_kv[0].reshape(rows, heads_here, HD)
    own_values = suffix_kv[1].reshape(rows, heads_here, HD).astype(jnp.float32)
    scores = (
        jnp.einsum("qhd,khd->hqk", queries, own_keys, preferred_element_type=jnp.float32) * scale
    )
    top = jnp.max(scores, axis=2)
    probs = jnp.exp(scores - top[:, :, None])
    total = jnp.sum(probs, axis=2)
    accum = jnp.einsum("hqk,khd->hqd", probs, own_values)
    my_nodes = path[0]
    node_ids = jnp.arange(node_len.shape[0], dtype=jnp.int32)
    if lax.axis_size("seq") <= DENSE_SEQ:
        owners = block_owners()
        piece = gather_blocks(prefix_kv).transpose(3, 0, 1, 2, 4, 5)
        piece = piece.reshape(2, -1, prefix_kv.shape[2])
    else:
        owners = node_ids
        piece = lax.all_gather(prefix_kv, "seq", axis=1, tiled=True)
    start = jnp.int32(0)
    count = piece.shape[1]

    def absorb(state):
        best, mass, sums = state
        index = jnp.arange(count, dtype=jnp.int32)
        node = jnp.repeat(owners, SLOT)
        offset = index % SLOT
        match = node[:, None] == node_ids[None, :]
        lengths = jnp.sum(jnp.where(match, node_len[None, :], 0), axis=1)
        live = (offset < lengths) & jnp.any(node[:, None] == my_nodes[None, :], axis=1)
        piece_keys = piece[0].reshape(count, heads_here, HD)
        piece_values = piece[1].reshape(count, heads_here, HD).astype(jnp.float32)
        block = (
            jnp.einsum("qhd,khd->hqk", queries, piece_keys, preferred_element_type=jnp.float32)
            * scale
        )
        block = jnp.where(live[None, None, :], block, -jnp.inf)
        new_best = jnp.maximum(best, jnp.max(block, axis=2))
        weights = jnp.exp(block - new_best[:, :, None])
        factor = jnp.exp(best - new_best)
        new_mass = mass * factor + jnp.sum(weights, axis=2)
        new_sums = sums * factor[:, :, None] + jnp.einsum("hqk,khd->hqd", weights, piece_values)
        return (new_best, new_mass, new_sums)

    node_start = my_nodes * SLOT
    touched = jnp.any((node_start + SLOT > start) & (node_start < start + count))
    top, total, accum = lax.cond(touched, absorb, lambda state: state, (top, total, accum))
    attn = (accum / total[:, :, None]).astype(jnp.bfloat16)
    partial_value = jnp.einsum(
        "hqd,hdm->qm",
        attn,
        out_weight.reshape(heads_here, HD, D),
        preferred_element_type=jnp.float32,
    )
    tp_index = lax.axis_index("tp")
    tp_count = lax.axis_size("tp")
    half = D // tp_count
    experts = w_gate.shape[0] * lax.axis_size("seq")
    cap = 5 * rows * TOPK // (4 * experts)
    dest = slot_plan(expert_ids, experts, cap)
    hidden_state = layer_input.astype(jnp.float32) + lax.psum(partial_value, "tp")
    mean_square = jnp.mean(hidden_state * hidden_state, axis=1, keepdims=True)
    normed = (hidden_state * lax.rsqrt(mean_square + 1e-06) * norm_gain).astype(jnp.bfloat16)
    if lax.axis_size("seq") <= DENSE_SEQ:
        mixture = dense_experts(normed, expert_ids, gates, w_gate, w_up, w_down, tp_index, half)
        residual = lax.dynamic_slice_in_dim(hidden_state, tp_index * half, half, 1)
        return (residual + mixture).astype(jnp.bfloat16)
    spread = jnp.repeat(normed, TOPK, axis=0)
    outgoing = (
        jnp.zeros((experts * cap, D), jnp.bfloat16).at[dest].set(spread).reshape(experts, cap, D)
    )
    arrived = lax.all_to_all(outgoing, "seq", split_axis=0, concat_axis=0, tiled=True)
    sources = arrived.shape[0]
    items = arrived.shape[1]
    flat = arrived.reshape(sources * items, D)
    gate_part = jnp.dot(flat, w_gate[0], preferred_element_type=jnp.float32)
    up_part = jnp.dot(flat, w_up[0], preferred_element_type=jnp.float32)
    act = (jax.nn.silu(gate_part) * up_part).astype(jnp.bfloat16)
    terms = jnp.dot(act, w_down[0], preferred_element_type=jnp.float32).reshape(sources, items, D)
    summed = lax.psum_scatter(terms, "tp", scatter_dimension=2, tiled=True).astype(jnp.bfloat16)
    back = lax.all_to_all(summed, "seq", split_axis=0, concat_axis=0, tiled=True)
    residual = lax.dynamic_slice_in_dim(hidden_state, tp_index * half, half, 1)
    results = back.reshape(experts * cap, half)[dest].reshape(rows, TOPK, half).astype(jnp.float32)
    mixture = jnp.sum(gates[:, :, None] * results, axis=1)
    return (residual + mixture).astype(jnp.bfloat16)


def solution(mesh):
    in_specs = (
        P("seq", None),
        P("seq", "tp"),
        P(None, "seq", "tp"),
        P(None, "seq", "tp"),
        P(),
        P("seq", None),
        P("tp", None),
        P(),
        P("seq", None),
        P("seq", None),
        P("seq", None, "tp"),
        P("seq", None, "tp"),
        P("seq", "tp", None),
    )
    out_specs = P("seq", "tp")
    return jax.shard_map(local, mesh=mesh, in_specs=in_specs, out_specs=out_specs, check_vma=False)
```

```python
import math

import jax
import jax.numpy as jnp
from jax import lax
from jax.sharding import PartitionSpec as P

D = 2048
HD = 128
TOPK = 8
SLOT = 32
DENSE_SEQ = 16


def slot_plan(ids, experts, cap):
    flat = ids.reshape(-1)
    onehot = (flat[:, None] == jnp.arange(experts, dtype=jnp.int32)[None, :]).astype(jnp.int32)
    rank = jnp.sum(jnp.cumsum(onehot, axis=0) * onehot, axis=1) - 1
    return flat * cap + rank


def flip(value, bit):
    return lax.ppermute(value, "seq", [(i, i ^ bit) for i in range(DENSE_SEQ)])


def shift(value, step):
    return lax.ppermute(value, "seq", [(i, (i + 4 * step) % DENSE_SEQ) for i in range(DENSE_SEQ)])


def gather_blocks(part):
    planes = jnp.stack([part] + [shift(part, k) for k in range(1, 4)])
    half = part.shape[-1] // 2
    first, second = planes[..., :half], planes[..., half:]
    first = jnp.stack([first, flip(first, 1)], 1)
    second = jnp.stack([second, flip(second, 2)], 1)
    first = jnp.stack([first, flip(first, 2)], 1)
    second = jnp.stack([second, flip(second, 1)], 2)
    return jnp.concatenate([first, second], -1)


def block_owners():
    mine = lax.axis_index("seq")
    return jnp.stack(
        [(mine + DENSE_SEQ - 4 * k) % DENSE_SEQ ^ b for k in range(4) for b in range(4)]
    )


def add(a, b):
    return (a.astype(jnp.float32) + b.astype(jnp.float32)).astype(jnp.bfloat16)


def reduce_blocks(terms):
    half = terms.shape[-1] // 2
    first, second = terms[..., :half], terms[..., half:]
    first_x = flip(first[:, :, 1], 1)
    second_y = flip(second[:, 1], 2)
    first = add(first[:, :, 0], first_x)
    second = add(second[:, 0], second_y)
    first_y = flip(first[:, 1], 2)
    second_x = flip(second[:, 1], 1)
    first = add(first[:, 0], first_y)
    second = add(second[:, 0], second_x)
    sums = []
    for piece in (first, second):
        arrived = [shift(piece[k], -k) for k in range(1, 4)]
        sums.append(piece[0].astype(jnp.float32) + sum(a.astype(jnp.float32) for a in arrived))
    return jnp.concatenate(sums, -1)


def dense_experts(normed, expert_ids, gates, w_gate, w_up, w_down, tp_index, half):
    mine = lax.axis_index("seq")
    experts = lax.axis_size("seq")
    rows = normed.shape[0]
    named = expert_ids[:, :, None] == jnp.arange(experts, dtype=jnp.int32)[None, None, :]
    table = jnp.sum(jnp.where(named, gates[:, :, None], 0.0), axis=1)
    table = lax.all_gather(table, "seq", axis=0, tiled=True)
    weight = lax.dynamic_slice_in_dim(table, mine, 1, 1)
    weight = weight.reshape(experts, -1)[block_owners()].reshape(-1, 1)
    part = lax.dynamic_slice_in_dim(normed, tp_index * half, half, 1)
    column = gather_blocks(part).reshape(experts * rows, half)
    other = lax.ppermute(column, "tp", [(0, 1), (1, 0)])
    tokens = jnp.concatenate([column, other], 1)
    w_gate = jnp.where(tp_index == 0, w_gate[0], jnp.roll(w_gate[0], half, 0))
    w_up = jnp.where(tp_index == 0, w_up[0], jnp.roll(w_up[0], half, 0))
    gate_part = jnp.dot(tokens, w_gate, preferred_element_type=jnp.float32)
    up_part = jnp.dot(tokens, w_up, preferred_element_type=jnp.float32)
    act = (jax.nn.silu(gate_part) * up_part).astype(jnp.bfloat16)
    terms = jnp.dot(act, w_down[0], preferred_element_type=jnp.float32) * weight
    terms = lax.psum_scatter(terms.astype(jnp.bfloat16), "tp", scatter_dimension=1, tiled=True)
    return reduce_blocks(terms.reshape(4, 2, 2, rows, half))


def local(
    layer_input,
    query,
    suffix_kv,
    prefix_kv,
    node_len,
    path,
    out_weight,
    norm_gain,
    expert_ids,
    gates,
    w_gate,
    w_up,
    w_down,
):
    rows = query.shape[0]
    heads_here = query.shape[1] // HD
    scale = 1.0 / math.sqrt(HD)
    queries = query.reshape(rows, heads_here, HD)
    own_keys = suffix_kv[0].reshape(rows, heads_here, HD)
    own_values = suffix_kv[1].reshape(rows, heads_here, HD).astype(jnp.float32)
    scores = (
        jnp.einsum("qhd,khd->hqk", queries, own_keys, preferred_element_type=jnp.float32) * scale
    )
    top = jnp.max(scores, axis=2)
    probs = jnp.exp(scores - top[:, :, None])
    total = jnp.sum(probs, axis=2)
    accum = jnp.einsum("hqk,khd->hqd", probs, own_values)
    my_nodes = path[0]
    node_ids = jnp.arange(node_len.shape[0], dtype=jnp.int32)
    if lax.axis_size("seq") <= DENSE_SEQ:
        owners = block_owners()
        piece = gather_blocks(prefix_kv).transpose(3, 0, 1, 2, 4, 5)
        piece = piece.reshape(2, -1, prefix_kv.shape[2])
    else:
        owners = node_ids
        piece = lax.all_gather(prefix_kv, "seq", axis=1, tiled=True)
    start = jnp.int32(0)
    count = piece.shape[1]

    def absorb(state):
        best, mass, sums = state
        index = jnp.arange(count, dtype=jnp.int32)
        node = jnp.repeat(owners, SLOT)
        offset = index % SLOT
        match = node[:, None] == node_ids[None, :]
        lengths = jnp.sum(jnp.where(match, node_len[None, :], 0), axis=1)
        live = (offset < lengths) & jnp.any(node[:, None] == my_nodes[None, :], axis=1)
        piece_keys = piece[0].reshape(count, heads_here, HD)
        piece_values = piece[1].reshape(count, heads_here, HD).astype(jnp.float32)
        block = (
            jnp.einsum("qhd,khd->hqk", queries, piece_keys, preferred_element_type=jnp.float32)
            * scale
        )
        block = jnp.where(live[None, None, :], block, -jnp.inf)
        new_best = jnp.maximum(best, jnp.max(block, axis=2))
        weights = jnp.exp(block - new_best[:, :, None])
        factor = jnp.exp(best - new_best)
        new_mass = mass * factor + jnp.sum(weights, axis=2)
        new_sums = sums * factor[:, :, None] + jnp.einsum("hqk,khd->hqd", weights, piece_values)
        return (new_best, new_mass, new_sums)

    node_start = my_nodes * SLOT
    touched = jnp.any((node_start + SLOT > start) & (node_start < start + count))
    top, total, accum = lax.cond(touched, absorb, lambda state: state, (top, total, accum))
    attn = (accum / total[:, :, None]).astype(jnp.bfloat16)
    partial_value = jnp.einsum(
        "hqd,hdm->qm",
        attn,
        out_weight.reshape(heads_here, HD, D),
        preferred_element_type=jnp.float32,
    )
    tp_index = lax.axis_index("tp")
    tp_count = lax.axis_size("tp")
    half = D // tp_count
    experts = w_gate.shape[0] * lax.axis_size("seq")
    cap = 5 * rows * TOPK // (4 * experts)
    dest = slot_plan(expert_ids, experts, cap)
    hidden_state = layer_input.astype(jnp.float32) + lax.psum(partial_value, "tp")
    mean_square = jnp.mean(hidden_state * hidden_state, axis=1, keepdims=True)
    normed = (hidden_state * lax.rsqrt(mean_square + 1e-06) * norm_gain).astype(jnp.bfloat16)
    if lax.axis_size("seq") <= DENSE_SEQ:
        mixture = dense_experts(normed, expert_ids, gates, w_gate, w_up, w_down, tp_index, half)
        residual = lax.dynamic_slice_in_dim(hidden_state, tp_index * half, half, 1)
        return (residual + mixture).astype(jnp.bfloat16)
    spread = jnp.repeat(normed, TOPK, axis=0)
    outgoing = (
        jnp.zeros((experts * cap, D), jnp.bfloat16).at[dest].set(spread).reshape(experts, cap, D)
    )
    arrived = lax.all_to_all(outgoing, "seq", split_axis=0, concat_axis=0, tiled=True)
    sources = arrived.shape[0]
    items = arrived.shape[1]
    flat = arrived.reshape(sources * items, D)
    gate_part = jnp.dot(flat, w_gate[0], preferred_element_type=jnp.float32)
    up_part = jnp.dot(flat, w_up[0], preferred_element_type=jnp.float32)
    act = (jax.nn.silu(gate_part) * up_part).astype(jnp.bfloat16)
    terms = jnp.dot(act, w_down[0], preferred_element_type=jnp.float32).reshape(sources, items, D)
    summed = lax.psum_scatter(terms, "tp", scatter_dimension=2, tiled=True).astype(jnp.bfloat16)
    back = lax.all_to_all(summed, "seq", split_axis=0, concat_axis=0, tiled=True)
    residual = lax.dynamic_slice_in_dim(hidden_state, tp_index * half, half, 1)
    results = back.reshape(experts * cap, half)[dest].reshape(rows, TOPK, half).astype(jnp.float32)
    mixture = jnp.sum(gates[:, :, None] * results, axis=1)
    return (residual + mixture).astype(jnp.bfloat16)


def solution(mesh):
    in_specs = (
        P("seq", None),
        P("seq", "tp"),
        P(None, "seq", "tp"),
        P(None, "seq", "tp"),
        P(),
        P("seq", None),
        P("tp", None),
        P(),
        P("seq", None),
        P("seq", None),
        P("seq", None, "tp"),
        P("seq", None, "tp"),
        P("seq", "tp", None),
    )
    out_specs = P("seq", "tp")
    return jax.shard_map(local, mesh=mesh, in_specs=in_specs, out_specs=out_specs, check_vma=False)
```
